512 devices in a mesh: dp: 32 (over z_hi, y, x), shard: 16 (over z_lo, core).
Axes of the slice: x: 4, y: 4, z: 16 (z_hi: 2, z_lo: 8; z = z_hi * 8 + z_lo), core: 2. Of those that a mesh axis runs over, the one named last changes fastest.
Arguments:
- inputs: bfloat16 [8192, 8192], P('dp'), may hold values from -6 to 6
- cotangent: bfloat16 [2, 8192, 14336], P(None, 'dp', 'shard'), may hold values from -0.06591797 to 0.06591797
- subspace: bfloat16 [2, 8192, 256], P(None, 'dp'), may hold values from -0.0625 to 0.0625
- first_moment: float32 [2, 256, 14336], P(None, 'dp', 'shard'), may hold values from -2 to 2
- second_moment: float32 [2, 256, 14336], P(None, 'dp', 'shard'), may hold values from 0.0001 to 0.01
Outputs:
- update: bfloat16 [2, 8192, 14336], P(None, 'dp', 'shard')
- new_first: float32 [2, 256, 14336], P(None, 'dp', 'shard')
- new_second: float32 [2, 256, 14336], P(None, 'dp', 'shard')
The draws below stay inside these ranges and needn't reach their ends.
All inputs are finite; a program needn't handle non-finite values.
Results may differ from the reference program's by a relative error of at most 0.0057.
Values may be sent and summed in bfloat16 or wider, within the bound.
No kernel may reach another device: no remote copies, remote signals or barrier semaphores. Data moves between devices by JAX's collectives and lax.ppermute only.
A program may use at most 64 MiB of HBM per device.

```python
import math
import jax
import jax.numpy as jnp
from jax import lax

D = 8192
FF = 14336
RANK = 256
STEP = 10
TOKENS = 8192


def block_levels(rng, shape, pieces, smallest, largest):
    level, own = 1.0, jax.random.fold_in(rng, 6)
    for dim, blocks in pieces:
        heights = jnp.exp(jax.random.uniform(jax.random.fold_in(own, dim), (blocks,), jnp.float32, smallest / len(pieces), largest / len(pieces)))
        level = level * jnp.repeat(heights, shape[dim] // blocks).reshape([-1 if axis == dim else 1 for axis in range(len(shape))])
    return level


def scatter_about(rng, dims, scale, bound, cuts=(), held_as=jnp.bfloat16):
    factor_of = block_levels(rng, dims, cuts, -0.22, 0.18) if cuts else 1.0
    entries = jax.random.normal(rng, dims, jnp.float32) * scale * factor_of
    return jnp.minimum(jnp.maximum(entries, -bound), bound).astype(held_as)


def setup_inputs(seed: int = 0) -> dict:
    keys = jax.random.split(jax.random.key(seed), 6)
    return {
        "inputs": scatter_about(keys[0], (TOKENS, D), 1.0, 6.0, ((0, 32),)),
        "cotangent": scatter_about(keys[1], (2, TOKENS, FF), (TOKENS ** -0.5), 0.06591797, ((1, 32), (2, 16))),
        "subspace": scatter_about(keys[2], (2, D, RANK), D ** -0.5, 0.0625, ((1, 32),)),
        "first_moment": scatter_about(keys[3], (2, RANK, FF), 0.3, 2.0, ((1, 32), (2, 16)), jnp.float32),
        "second_moment": jnp.clip(jnp.exp(math.log(0.01) - 4.6051702 * jax.random.uniform(keys[4], (2, RANK, FF), jnp.float32) ** block_levels(keys[4], (2, RANK, FF), ((1, 32), (2, 16)), -0.2, 0.2)), 0.0001, 0.01),
    }


def reference(inputs, cotangent, subspace, first_moment, second_moment):
    highest = lax.Precision.HIGHEST
    projected = jnp.einsum('td,gdr->gtr', inputs.astype(jnp.float32), subspace.astype(jnp.float32), precision=highest).astype(jnp.bfloat16)
    gradient = jnp.einsum('gtr,gtf->grf', projected.astype(jnp.float32), cotangent.astype(jnp.float32), precision=highest)
    new_first = 0.9 * first_moment + 0.1 * gradient
    new_second = 0.999 * second_moment + 0.001 * gradient * gradient
    first_fix = 1.0 - 0.9 ** STEP
    second_fix = 1.0 - 0.999 ** STEP
    normalized = (new_first / first_fix / (jnp.sqrt(new_second / second_fix) + 1e-08)).astype(jnp.bfloat16)

    def project_back(pair):
        return jnp.dot(pair[0], pair[1], preferred_element_type=jnp.float32).astype(jnp.bfloat16)
    update = lax.map(project_back, (subspace, normalized))
    return (update, new_first, new_second)
```

```python
import jax
import jax.numpy as jnp
from jax import lax
from jax.sharding import Mesh, PartitionSpec as P

STEP = 10
PLANE = ("y", "x")
LINE = ("zl", "c")


def per_device(inputs, cotangent, subspace, first_moment, second_moment):
    f32, bf16 = jnp.float32, jnp.bfloat16
    swap = [(0, 1), (1, 0)]
    moments = jnp.stack([first_moment, second_moment])
    moments_far = lax.ppermute(moments, "zh", swap)

    ranks = subspace.reshape(2, 256, 2, 16, 8).transpose(3, 0, 2, 4, 1)
    place = lax.axis_index(LINE)
    mine = lax.dynamic_index_in_dim(ranks, place, 0, keepdims=False).reshape(32, 256)
    other = lax.ppermute(mine, "zh", swap)
    half = lax.axis_index("zh")
    both = jnp.where(half == 0, jnp.stack([mine, other]), jnp.stack([other, mine]))
    basis = lax.all_to_all(
        jnp.broadcast_to(both, (16, 2, 32, 256)), PLANE, 0, 0, tiled=True
    )
    basis = basis.transpose(2, 1, 0, 3).reshape(32, 8192)
    projected = lax.dot_general(
        basis, inputs, (((1,), (1,)), ((), ())), preferred_element_type=f32
    ).astype(bf16)
    projected = lax.all_to_all(
        jnp.broadcast_to(projected, (8, 32, 256)), "zl", 0, 0, tiled=True
    )
    projected = lax.all_gather(projected, "c", axis=1).reshape(16, 2, 2, 8, 256)
    partial = jnp.einsum(
        "yghkt,gtc->yghkc", projected, cotangent, preferred_element_type=f32
    ).astype(bf16)
    parts = lax.all_to_all(partial, PLANE, 0, 0, tiled=True)
    own = jnp.sum(parts.astype(f32), axis=0)
    far = lax.ppermute(own.astype(bf16), "zh", swap)
    gradient = own + far.astype(f32)

    near_far = jnp.stack([moments, moments_far], axis=2)
    far_near = jnp.stack([moments_far, moments], axis=2)
    held = jnp.where(half == 0, near_far, far_near)
    new_first = 0.9 * held[0] + 0.1 * gradient
    new_second = 0.999 * held[1] + 0.001 * gradient * gradient
    first_fix = 1.0 - 0.9**STEP
    second_fix = 1.0 - 0.999**STEP
    normalized = (new_first / first_fix / (jnp.sqrt(new_second / second_fix) + 1e-08)).astype(bf16)
    steps = lax.all_to_all(
        jnp.broadcast_to(normalized, (16, 2, 2, 8, 896)), PLANE, 0, 0, tiled=True
    )
    update = jnp.einsum(
        "yghkd,yghkc->gdc", ranks, steps, preferred_element_type=f32
    ).astype(bf16)
    return (
        update,
        jnp.where(half == 0, new_first[:, 0], new_first[:, 1]),
        jnp.where(half == 0, new_second[:, 0], new_second[:, 1]),
    )


def solution(mesh):
    fine = Mesh(mesh.devices.reshape(2, 4, 4, 8, 2), ("zh", "y", "x", "zl", "c"))
    dp, shard = ("zh", "y", "x"), ("zl", "c")
    return jax.shard_map(
        per_device,
        mesh=fine,
        in_specs=(
            P(dp, None),
            P(None, dp, shard),
            P(None, dp, None),
            P(None, dp, shard),
            P(None, dp, shard),
        ),
        out_specs=(P(None, dp, shard), P(None, dp, shard), P(None, dp, shard)),
        check_vma=False,
    )
```

```python
import jax
import jax.numpy as jnp
from jax import lax
from jax.experimental import pallas as pl
from jax.experimental.pallas import tpu as pltpu
from jax.sharding import Mesh, PartitionSpec as P

STEP = 10
PLANE = ("y", "x")
LINE = ("z_hi", "z_top", "z_mid", "z_lo")
NEAR = ("z_mid", "z_lo")
SWAP = [(0, 1), (1, 0)]
f32, bf16 = jnp.float32, jnp.bfloat16


def spread(block, axes, count):
    return lax.all_to_all(
        jnp.broadcast_to(block, (count, *block.shape)), axes, 0, 0, tiled=True
    )


def in_vmem(kernel, out, name, *operands):
    spec = pl.BlockSpec(memory_space=pltpu.VMEM)
    return pl.pallas_call(
        kernel,
        in_specs=[spec] * len(operands),
        out_specs=jax.tree.map(lambda _: spec, out),
        out_shape=out,
        compiler_params=pltpu.CompilerParams(vmem_limit_bytes=16 * 2**20),
        name=name,
    )(*operands)


def fetch_kernel(column_ref, inputs_ref, out_ref, sem):
    column = pl.multiple_of(column_ref[0], 4096)
    copy = pltpu.make_async_copy(inputs_ref.at[:, pl.ds(column, 4096)], out_ref, sem)
    copy.start()
    copy.wait()


def fetch(inputs, column):
    return pl.pallas_call(
        fetch_kernel,
        in_specs=[
            pl.BlockSpec(memory_space=pltpu.SMEM),
            pl.BlockSpec(memory_space=pl.ANY),
        ],
        out_specs=pl.BlockSpec(memory_space=pltpu.VMEM),
        out_shape=jax.ShapeDtypeStruct((256, 4096), bf16),
        scratch_shapes=[pltpu.SemaphoreType.DMA],
        compiler_params=pltpu.CompilerParams(vmem_limit_bytes=16 * 2**20),
        name="fetch",
    )(column.reshape(1), inputs)


def project_kernel(basis_ref, inputs_ref, out_ref):
    acc = jnp.zeros((256, 128), f32)
    for place in range(16):
        acc += jnp.dot(
            inputs_ref[:, place * 256 : (place + 1) * 256],
            basis_ref[place],
            preferred_element_type=f32,
        )
    out_ref[...] = jnp.broadcast_to(acc.T.astype(bf16), (4, 128, 256))


def gradient_kernel(halves_ref, cotangent_ref, out_ref):
    for g in range(2):
        both = halves_ref[g, 0].astype(f32) + halves_ref[g, 1].astype(f32)
        part = jnp.dot(both.astype(bf16), cotangent_ref[g], preferred_element_type=f32)
        out_ref[:, g] = part.astype(bf16).reshape(16, 16, 896)


def update_kernel(basis_ref, steps_ref, gradient_ref, first_ref, second_ref, *refs):
    outs, (update, first, second, sems) = refs[:3], refs[3:]
    gradient = gradient_ref[...]
    first[...] = 0.9 * first_ref[...] + 0.1 * gradient
    second[...] = 0.999 * second_ref[...] + 0.001 * gradient * gradient
    copies = [
        pltpu.make_async_copy(first, outs[1], sems.at[2]),
        pltpu.make_async_copy(second, outs[2], sems.at[3]),
    ]
    for copy in copies:
        copy.start()
    for g in range(2):
        steps = steps_ref[:, g].reshape(256, 896)
        update[g] = jnp.dot(basis_ref[g], steps, preferred_element_type=f32).astype(bf16)
        copies.append(pltpu.make_async_copy(update.at[g], outs[0].at[g], sems.at[g]))
        copies[-1].start()
    for copy in copies:
        copy.wait()


def finish(basis, steps, gradient, first_moment, second_moment):
    outs = (
        jax.ShapeDtypeStruct((2, 256, 896), bf16),
        jax.ShapeDtypeStruct((2, 8, 896), f32),
        jax.ShapeDtypeStruct((2, 8, 896), f32),
    )
    return pl.pallas_call(
        update_kernel,
        in_specs=[pl.BlockSpec(memory_space=pltpu.VMEM)] * 5,
        out_specs=(pl.BlockSpec(memory_space=pl.ANY),) * 3,
        out_shape=outs,
        scratch_shapes=[
            *(pltpu.VMEM(out.shape, out.dtype) for out in outs),
            pltpu.SemaphoreType.DMA((4,)),
        ],
        compiler_params=pltpu.CompilerParams(vmem_limit_bytes=16 * 2**20),
        name="finish",
    )(basis, steps, gradient, first_moment, second_moment)


def per_device(inputs, cotangent, subspace, first_moment, second_moment):
    half, core = lax.axis_index("z_hi"), lax.axis_index("core")
    low = lax.axis_index("z_lo")
    across = lax.axis_index("z_mid") == lax.axis_index("z_top")

    order = lax.broadcasted_iota(jnp.int32, (256,), 0)
    order = order // 8 % 2 * 128 + order // 16 * 8 + order % 8
    wanted = lax.dynamic_slice(order, (jnp.where(across, 1 - low, low) * 128,), (128,))
    every = lax.broadcasted_iota(jnp.int32, (128, 256), 1)
    pick = (wanted[:, None] == every).astype(bf16)
    chosen = lax.dynamic_index_in_dim(subspace, core, 0, keepdims=False)
    mine = jnp.einsum("dr,sr->ds", chosen, pick, preferred_element_type=f32).astype(bf16)
    theirs = lax.ppermute(mine, LINE, [(z, 15 - z) for z in (0, 1, 6, 7, 8, 9, 14, 15)])
    moments = jnp.stack([first_moment, second_moment])
    moments_far = lax.ppermute(moments, "z_hi", SWAP)
    features = jnp.where(across, 1 - half, half) * 4096
    held = fetch(inputs, features)
    basis = jnp.where(across, theirs, mine)
    basis, held = lax.optimization_barrier((basis, held))

    basis = spread(basis, PLANE, 16)
    projected = in_vmem(
        project_kernel, jax.ShapeDtypeStruct((4, 128, 256), bf16), "project", basis, held
    )
    projected = lax.all_to_all(projected, NEAR, 0, 0, tiled=True)
    projected = lax.all_gather(projected, "core", axis=0).reshape(2, 2, 256, 256)
    partial = in_vmem(
        gradient_kernel,
        jax.ShapeDtypeStruct((16, 2, 16, 896), bf16),
        "gradient_parts",
        projected,
        cotangent,
    )
    parts = lax.all_to_all(partial, PLANE, 0, 0, tiled=True)
    own = jnp.sum(parts.astype(f32), axis=0).reshape(2, 2, 8, 896)
    far = lax.ppermute(own.astype(bf16), "z_hi", SWAP)
    after, _ = lax.optimization_barrier((subspace, own))
    move = (order[:, None] == lax.broadcasted_iota(jnp.int32, (256, 256), 1)).astype(bf16)
    ordered = jnp.einsum("gdr,sr->gds", after, move, preferred_element_type=f32).astype(bf16)
    gradient = own + far.astype(f32)

    near_far = jnp.stack([moments, moments_far], axis=2)
    far_near = jnp.stack([moments_far, moments], axis=2)
    held = jnp.where(half == 0, near_far, far_near)
    first_fix = 1.0 - 0.9**STEP
    second_fix = 1.0 - 0.999**STEP
    new_first = 0.9 * held[0] + 0.1 * gradient
    new_second = 0.999 * held[1] + 0.001 * gradient * gradient
    normalized = new_first / first_fix / (jnp.sqrt(new_second / second_fix) + 1e-08)
    gradient = lax.dynamic_index_in_dim(gradient, half, 1, keepdims=False)
    normalized, gradient, ordered = lax.optimization_barrier(
        (normalized.astype(bf16).reshape(2, 16, 896), gradient, ordered)
    )
    steps = spread(normalized, PLANE, 16)
    return finish(ordered, steps, gradient, first_moment, second_moment)


def solution(mesh):
    fine = Mesh(
        mesh.devices.reshape(2, 4, 4, 2, 2, 2, 2),
        ("z_hi", "y", "x", "z_top", "z_mid", "z_lo", "core"),
    )
    dp, shard = ("z_hi", "y", "x"), ("z_top", "z_mid", "z_lo", "core")
    return jax.shard_map(
        per_device,
        mesh=fine,
        in_specs=(
            P(dp, None),
            P(None, dp, shard),
            P(None, dp, None),
            P(None, dp, shard),
            P(None, dp, shard),
        ),
        out_specs=(P(None, dp, shard), P(None, dp, shard), P(None, dp, shard)),
        check_vma=False,
    )
```

```python
import jax
import jax.numpy as jnp
from jax import lax
from jax.experimental import pallas as pl
from jax.experimental.pallas import tpu as pltpu
from jax.sharding import Mesh, PartitionSpec as P

STEP = 10
PLANE = ("y", "x")
LINE = ("z_hi", "z_top", "z_mid", "z_lo")
NEAR = ("z_mid", "z_lo")
SWAP = [(0, 1), (1, 0)]
f32, bf16 = jnp.float32, jnp.bfloat16


def spread(block, axes, count):
    return lax.all_to_all(
        jnp.broadcast_to(block, (count, *block.shape)), axes, 0, 0, tiled=True
    )


def in_vmem(kernel, out, name, *operands):
    spec = pl.BlockSpec(memory_space=pltpu.VMEM)
    return pl.pallas_call(
        kernel,
        in_specs=[spec] * len(operands),
        out_specs=jax.tree.map(lambda _: spec, out),
        out_shape=out,
        compiler_params=pltpu.CompilerParams(vmem_limit_bytes=16 * 2**20),
        name=name,
    )(*operands)


def fetch_kernel(column_ref, inputs_ref, out_ref, sem):
    column = pl.multiple_of(column_ref[0], 4096)
    copy = pltpu.make_async_copy(inputs_ref.at[:, pl.ds(column, 4096)], out_ref, sem)
    copy.start()
    copy.wait()


def fetch(inputs, column):
    return pl.pallas_call(
        fetch_kernel,
        in_specs=[
            pl.BlockSpec(memory_space=pltpu.SMEM),
            pl.BlockSpec(memory_space=pl.ANY),
        ],
        out_specs=pl.BlockSpec(memory_space=pltpu.VMEM),
        out_shape=jax.ShapeDtypeStruct((256, 4096), bf16),
        scratch_shapes=[pltpu.SemaphoreType.DMA],
        compiler_params=pltpu.CompilerParams(vmem_limit_bytes=16 * 2**20),
        name="fetch",
    )(column.reshape(1), inputs)


def project_kernel(basis_ref, inputs_ref, out_ref):
    acc = jnp.zeros((256, 128), f32)
    for place in range(16):
        acc += jnp.dot(
            inputs_ref[:, place * 256 : (place + 1) * 256],
            basis_ref[place],
            preferred_element_type=f32,
        )
    out_ref[...] = jnp.broadcast_to(acc.T.astype(bf16), (4, 128, 256))


def gradient_kernel(halves_ref, cotangent_ref, out_ref, parts, sems):
    copies = []
    for g in range(2):
        both = halves_ref[g, 0].astype(f32) + halves_ref[g, 1].astype(f32)
        both = both.astype(bf16)
        for piece in range(2):
            rows = slice(piece * 8, piece * 8 + 8)
            part = jnp.dot(
                both[piece * 128 : piece * 128 + 128],
                cotangent_ref[g],
                preferred_element_type=f32,
            )
            parts[rows, g] = part.astype(bf16).reshape(8, 16, 896)
            copies.append(
                pltpu.make_async_copy(
                    parts.at[rows, g], out_ref.at[rows, g], sems.at[2 * g + piece]
                )
            )
            copies[-1].start()
    for copy in copies:
        copy.wait()


def gradient_parts(halves, cotangent):
    out = jax.ShapeDtypeStruct((16, 2, 16, 896), bf16)
    return pl.pallas_call(
        gradient_kernel,
        in_specs=[pl.BlockSpec(memory_space=pltpu.VMEM)] * 2,
        out_specs=pl.BlockSpec(memory_space=pl.ANY),
        out_shape=out,
        scratch_shapes=[pltpu.VMEM(out.shape, bf16), pltpu.SemaphoreType.DMA((4,))],
        compiler_params=pltpu.CompilerParams(vmem_limit_bytes=16 * 2**20),
        name="gradient_parts",
    )(halves, cotangent)


def update_kernel(basis_ref, steps_ref, gradient_ref, first_ref, second_ref, *refs):
    outs, (update, first, second, sems) = refs[:3], refs[3:]
    gradient = gradient_ref[...]
    first[...] = 0.9 * first_ref[...] + 0.1 * gradient
    second[...] = 0.999 * second_ref[...] + 0.001 * gradient * gradient
    copies = [
        pltpu.make_async_copy(first, outs[1], sems.at[4]),
        pltpu.make_async_copy(second, outs[2], sems.at[5]),
    ]
    for copy in copies:
        copy.start()
    for g in range(2):
        steps = steps_ref[:, g].reshape(256, 896)
        for piece in range(2):
            rows = slice(piece * 128, piece * 128 + 128)
            update[g, rows] = jnp.dot(
                basis_ref[g, rows], steps, preferred_element_type=f32
            ).astype(bf16)
            copies.append(
                pltpu.make_async_copy(
                    update.at[g, rows], outs[0].at[g, rows], sems.at[2 * g + piece]
                )
            )
            copies[-1].start()
    for copy in copies:
        copy.wait()


def finish(basis, steps, gradient, first_moment, second_moment):
    outs = (
        jax.ShapeDtypeStruct((2, 256, 896), bf16),
        jax.ShapeDtypeStruct((2, 8, 896), f32),
        jax.ShapeDtypeStruct((2, 8, 896), f32),
    )
    return pl.pallas_call(
        update_kernel,
        in_specs=[pl.BlockSpec(memory_space=pltpu.VMEM)] * 5,
        out_specs=(pl.BlockSpec(memory_space=pl.ANY),) * 3,
        out_shape=outs,
        scratch_shapes=[
            *(pltpu.VMEM(out.shape, out.dtype) for out in outs),
            pltpu.SemaphoreType.DMA((6,)),
        ],
        compiler_params=pltpu.CompilerParams(vmem_limit_bytes=16 * 2**20),
        name="finish",
    )(basis, steps, gradient, first_moment, second_moment)


def per_device(inputs, cotangent, subspace, first_moment, second_moment):
    half, core = lax.axis_index("z_hi"), lax.axis_index("core")
    low = lax.axis_index("z_lo")
    across = lax.axis_index("z_mid") == lax.axis_index("z_top")

    order = lax.broadcasted_iota(jnp.int32, (256,), 0)
    order = order // 8 % 2 * 128 + order // 16 * 8 + order % 8
    wanted = lax.dynamic_slice(order, (jnp.where(across, 1 - low, low) * 128,), (128,))
    every = lax.broadcasted_iota(jnp.int32, (128, 256), 1)
    pick = (wanted[:, None] == every).astype(bf16)
    chosen = lax.dynamic_index_in_dim(subspace, core, 0, keepdims=False)
    mine = jnp.einsum("dr,sr->ds", chosen, pick, preferred_element_type=f32).astype(bf16)
    theirs = lax.ppermute(mine, LINE, [(z, 15 - z) for z in (0, 1, 6, 7, 8, 9, 14, 15)])
    moments = jnp.stack([first_moment, second_moment])
    moments_far = lax.ppermute(moments, "z_hi", SWAP)
    features = jnp.where(across, 1 - half, half) * 4096
    held = fetch(inputs, features)
    basis = jnp.where(across, theirs, mine)
    basis, held = lax.optimization_barrier((basis, held))

    basis = spread(basis, PLANE, 16)
    projected = in_vmem(
        project_kernel, jax.ShapeDtypeStruct((4, 128, 256), bf16), "project", basis, held
    )
    projected = lax.all_to_all(projected, NEAR, 0, 0, tiled=True)
    projected = lax.all_gather(projected, "core", axis=0).reshape(2, 2, 256, 256)
    partial = gradient_parts(projected, cotangent)
    parts = lax.all_to_all(partial, PLANE, 0, 0, tiled=True)
    own = jnp.sum(parts.astype(f32), axis=0).reshape(2, 2, 8, 896)
    sums = lax.all_gather(own.astype(bf16), "z_hi", axis=0)
    sums, moments_far = lax.optimization_barrier((sums, moments_far))
    after, _ = lax.optimization_barrier((subspace, own))
    move = (order[:, None] == lax.broadcasted_iota(jnp.int32, (256, 256), 1)).astype(bf16)
    ordered = jnp.einsum("gdr,sr->gds", after, move, preferred_element_type=f32).astype(bf16)
    gradient = own + jnp.where(half == 0, sums[1], sums[0]).astype(f32)

    near_far = jnp.stack([moments, moments_far], axis=2)
    far_near = jnp.stack([moments_far, moments], axis=2)
    held = jnp.where(half == 0, near_far, far_near)
    first_fix = 1.0 - 0.9**STEP
    second_fix = 1.0 - 0.999**STEP
    new_first = 0.9 * held[0] + 0.1 * gradient
    new_second = 0.999 * held[1] + 0.001 * gradient * gradient
    normalized = new_first / first_fix / (jnp.sqrt(new_second / second_fix) + 1e-08)
    gradient = lax.dynamic_index_in_dim(gradient, half, 1, keepdims=False)
    normalized, gradient, ordered = lax.optimization_barrier(
        (normalized.astype(bf16).reshape(2, 16, 896), gradient, ordered)
    )
    steps = spread(normalized, PLANE, 16)
    return finish(ordered, steps, gradient, first_moment, second_moment)


def solution(mesh):
    fine = Mesh(
        mesh.devices.reshape(2, 4, 4, 2, 2, 2, 2),
        ("z_hi", "y", "x", "z_top", "z_mid", "z_lo", "core"),
    )
    dp, shard = ("z_hi", "y", "x"), ("z_top", "z_mid", "z_lo", "core")
    return jax.shard_map(
        per_device,
        mesh=fine,
        in_specs=(
            P(dp, None),
            P(None, dp, shard),
            P(None, dp, None),
            P(None, dp, shard),
            P(None, dp, shard),
        ),
        out_specs=(P(None, dp, shard), P(None, dp, shard), P(None, dp, shard)),
        check_vma=False,
    )
```

```python
import jax
import jax.numpy as jnp
from jax import lax
from jax.experimental import pallas as pl
from jax.experimental.pallas import tpu as pltpu
from jax.sharding import Mesh, PartitionSpec as P

STEP = 10
PLANE = ("y", "x")
LINE = ("z_hi", "z_top", "z_mid", "z_lo")
NEAR = ("z_mid", "z_lo")
SWAP = [(0, 1), (1, 0)]
f32, bf16 = jnp.float32, jnp.bfloat16


def spread(block, axes, count):
    return lax.all_to_all(
        jnp.broadcast_to(block, (count, *block.shape)), axes, 0, 0, tiled=True
    )


def in_vmem(kernel, out, name, *operands):
    spec = pl.BlockSpec(memory_space=pltpu.VMEM)
    return pl.pallas_call(
        kernel,
        in_specs=[spec] * len(operands),
        out_specs=jax.tree.map(lambda _: spec, out),
        out_shape=out,
        compiler_params=pltpu.CompilerParams(vmem_limit_bytes=16 * 2**20),
        name=name,
    )(*operands)


def fetch_kernel(column_ref, inputs_ref, out_ref, sem):
    column = pl.multiple_of(column_ref[0], 4096)
    copy = pltpu.make_async_copy(inputs_ref.at[:, pl.ds(column, 4096)], out_ref, sem)
    copy.start()
    copy.wait()


def fetch(inputs, column):
    return pl.pallas_call(
        fetch_kernel,
        in_specs=[
            pl.BlockSpec(memory_space=pltpu.SMEM),
            pl.BlockSpec(memory_space=pl.ANY),
        ],
        out_specs=pl.BlockSpec(memory_space=pltpu.VMEM),
        out_shape=jax.ShapeDtypeStruct((256, 4096), bf16),
        scratch_shapes=[pltpu.SemaphoreType.DMA],
        compiler_params=pltpu.CompilerParams(vmem_limit_bytes=16 * 2**20),
        name="fetch",
    )(column.reshape(1), inputs)


def project_kernel(basis_ref, inputs_ref, out_ref):
    acc = jnp.zeros((256, 128), f32)
    for place in range(16):
        acc += jnp.dot(
            inputs_ref[:, place * 256 : (place + 1) * 256],
            basis_ref[place],
            preferred_element_type=f32,
        )
    out_ref[...] = jnp.broadcast_to(acc.T.astype(bf16), (4, 128, 256))


def gradient_kernel(halves_ref, cotangent_ref, out_ref, parts, sems):
    copies = []
    for g in range(2):
        both = halves_ref[g, 0].astype(f32) + halves_ref[g, 1].astype(f32)
        both = both.astype(bf16)
        for piece in range(2):
            rows = slice(piece * 8, piece * 8 + 8)
            part = jnp.dot(
                both[piece * 128 : piece * 128 + 128],
                cotangent_ref[g],
                preferred_element_type=f32,
            )
            parts[rows, g] = part.astype(bf16).reshape(8, 16, 896)
            copies.append(
                pltpu.make_async_copy(
                    parts.at[rows, g], out_ref.at[rows, g], sems.at[2 * g + piece]
                )
            )
            copies[-1].start()
    for copy in copies:
        copy.wait()


def gradient_parts(halves, cotangent):
    out = jax.ShapeDtypeStruct((16, 2, 16, 896), bf16)
    return pl.pallas_call(
        gradient_kernel,
        in_specs=[pl.BlockSpec(memory_space=pltpu.VMEM)] * 2,
        out_specs=pl.BlockSpec(memory_space=pl.ANY),
        out_shape=out,
        scratch_shapes=[pltpu.VMEM(out.shape, bf16), pltpu.SemaphoreType.DMA((4,))],
        compiler_params=pltpu.CompilerParams(vmem_limit_bytes=16 * 2**20),
        name="gradient_parts",
    )(halves, cotangent)


def update_kernel(basis_ref, steps_ref, gradient_ref, first_ref, second_ref, *refs):
    outs, (update, first, second, sems) = refs[:3], refs[3:]
    gradient = gradient_ref[...]
    first[...] = 0.9 * first_ref[...] + 0.1 * gradient
    second[...] = 0.999 * second_ref[...] + 0.001 * gradient * gradient
    copies = [
        pltpu.make_async_copy(first, outs[1], sems.at[4]),
        pltpu.make_async_copy(second, outs[2], sems.at[5]),
    ]
    for copy in copies:
        copy.start()
    for g in range(2):
        steps = steps_ref[:, g].reshape(256, 896)
        for piece in range(2):
            rows = slice(piece * 128, piece * 128 + 128)
            update[g, rows] = jnp.dot(
                basis_ref[g, rows], steps, preferred_element_type=f32
            ).astype(bf16)
            copies.append(
                pltpu.make_async_copy(
                    update.at[g, rows], outs[0].at[g, rows], sems.at[2 * g + piece]
                )
            )
            copies[-1].start()
    for copy in copies:
        copy.wait()


def finish(basis, steps, gradient, first_moment, second_moment):
    outs = (
        jax.ShapeDtypeStruct((2, 256, 896), bf16),
        jax.ShapeDtypeStruct((2, 8, 896), f32),
        jax.ShapeDtypeStruct((2, 8, 896), f32),
    )
    return pl.pallas_call(
        update_kernel,
        in_specs=[pl.BlockSpec(memory_space=pltpu.VMEM)] * 5,
        out_specs=(pl.BlockSpec(memory_space=pl.ANY),) * 3,
        out_shape=outs,
        scratch_shapes=[
            *(pltpu.VMEM(out.shape, out.dtype) for out in outs),
            pltpu.SemaphoreType.DMA((6,)),
        ],
        compiler_params=pltpu.CompilerParams(vmem_limit_bytes=16 * 2**20),
        name="finish",
    )(basis, steps, gradient, first_moment, second_moment)


def per_device(inputs, cotangent, subspace, first_moment, second_moment):
    half, core = lax.axis_index("z_hi"), lax.axis_index("core")
    low = lax.axis_index("z_lo")
    across = lax.axis_index("z_mid") == lax.axis_index("z_top")

    order = lax.broadcasted_iota(jnp.int32, (256,), 0)
    order = order // 8 % 2 * 128 + order // 16 * 8 + order % 8
    wanted = lax.dynamic_slice(order, (jnp.where(across, 1 - low, low) * 128,), (128,))
    every = lax.broadcasted_iota(jnp.int32, (128, 256), 1)
    pick = (wanted[:, None] == every).astype(bf16)
    chosen = lax.dynamic_index_in_dim(subspace, core, 0, keepdims=False)
    mine = jnp.einsum("dr,sr->ds", chosen, pick, preferred_element_type=f32).astype(bf16)
    theirs = lax.ppermute(mine, LINE, [(z, 15 - z) for z in (0, 1, 6, 7, 8, 9, 14, 15)])
    moments = jnp.stack([first_moment, second_moment])
    moments_far = lax.ppermute(moments.astype(bf16), "z_hi", SWAP)
    features = jnp.where(across, 1 - half, half) * 4096
    held = fetch(inputs, features)
    basis = jnp.where(across, theirs, mine)
    basis, held = lax.optimization_barrier((basis, held))

    basis = spread(basis, PLANE, 16)
    projected = in_vmem(
        project_kernel, jax.ShapeDtypeStruct((4, 128, 256), bf16), "project", basis, held
    )
    projected = lax.all_to_all(projected, NEAR, 0, 0, tiled=True)
    projected = lax.all_gather(projected, "core", axis=0).reshape(2, 2, 256, 256)
    partial = gradient_parts(projected, cotangent)
    parts = lax.all_to_all(partial, PLANE, 0, 0, tiled=True)
    own = jnp.sum(parts.astype(f32), axis=0).reshape(2, 2, 8, 896)
    sums = lax.all_gather(own.astype(bf16), "z_hi", axis=0)
    sums, moments_far = lax.optimization_barrier((sums, moments_far))
    moments_far = moments_far.astype(f32)
    after, _ = lax.optimization_barrier((subspace, own))
    move = (order[:, None] == lax.broadcasted_iota(jnp.int32, (256, 256), 1)).astype(bf16)
    ordered = jnp.einsum("gdr,sr->gds", after, move, preferred_element_type=f32).astype(bf16)
    gradient = own + jnp.where(half == 0, sums[1], sums[0]).astype(f32)

    near_far = jnp.stack([moments, moments_far], axis=2)
    far_near = jnp.stack([moments_far, moments], axis=2)
    held = jnp.where(half == 0, near_far, far_near)
    first_fix = 1.0 - 0.9**STEP
    second_fix = 1.0 - 0.999**STEP
    new_first = 0.9 * held[0] + 0.1 * gradient
    new_second = 0.999 * held[1] + 0.001 * gradient * gradient
    normalized = new_first / first_fix / (jnp.sqrt(new_second / second_fix) + 1e-08)
    gradient = lax.dynamic_index_in_dim(gradient, half, 1, keepdims=False)
    normalized, gradient, ordered = lax.optimization_barrier(
        (normalized.astype(bf16).reshape(2, 16, 896), gradient, ordered)
    )
    steps = spread(normalized, PLANE, 16)
    return finish(ordered, steps, gradient, first_moment, second_moment)


def solution(mesh):
    fine = Mesh(
        mesh.devices.reshape(2, 4, 4, 2, 2, 2, 2),
        ("z_hi", "y", "x", "z_top", "z_mid", "z_lo", "core"),
    )
    dp, shard = ("z_hi", "y", "x"), ("z_top", "z_mid", "z_lo", "core")
    return jax.shard_map(
        per_device,
        mesh=fine,
        in_specs=(
            P(dp, None),
            P(None, dp, shard),
            P(None, dp, None),
            P(None, dp, shard),
            P(None, dp, shard),
        ),
        out_specs=(P(None, dp, shard), P(None, dp, shard), P(None, dp, shard)),
        check_vma=False,
    )
```

```python
import jax
import jax.numpy as jnp
from jax import lax
from jax.experimental import pallas as pl
from jax.experimental.pallas import tpu as pltpu
from jax.sharding import Mesh, PartitionSpec as P

STEP = 10
PLANE = ("y", "x")
LINE = ("z_hi", "z_top", "z_mid", "z_lo")
NEAR = ("z_mid", "z_lo")
SWAP = [(0, 1), (1, 0)]
f32, bf16 = jnp.float32, jnp.bfloat16


def spread(block, axes, count):
    return lax.all_to_all(
        jnp.broadcast_to(block, (count, *block.shape)), axes, 0, 0, tiled=True
    )


def in_vmem(kernel, out, name, *operands):
    spec = pl.BlockSpec(memory_space=pltpu.VMEM)
    return pl.pallas_call(
        kernel,
        in_specs=[spec] * len(operands),
        out_specs=jax.tree.map(lambda _: spec, out),
        out_shape=out,
        compiler_params=pltpu.CompilerParams(vmem_limit_bytes=16 * 2**20),
        name=name,
    )(*operands)


def fetch_kernel(column_ref, inputs_ref, out_ref, sem):
    column = pl.multiple_of(column_ref[0], 4096)
    copy = pltpu.make_async_copy(inputs_ref.at[:, pl.ds(column, 4096)], out_ref, sem)
    copy.start()
    copy.wait()


def fetch(inputs, column):
    return pl.pallas_call(
        fetch_kernel,
        in_specs=[
            pl.BlockSpec(memory_space=pltpu.SMEM),
            pl.BlockSpec(memory_space=pl.ANY),
        ],
        out_specs=pl.BlockSpec(memory_space=pltpu.VMEM),
        out_shape=jax.ShapeDtypeStruct((256, 4096), bf16),
        scratch_shapes=[pltpu.SemaphoreType.DMA],
        compiler_params=pltpu.CompilerParams(vmem_limit_bytes=16 * 2**20),
        name="fetch",
    )(column.reshape(1), inputs)


def project_kernel(basis_ref, inputs_ref, out_ref):
    acc = jnp.zeros((256, 128), f32)
    for place in range(16):
        acc += jnp.dot(
            inputs_ref[:, place * 256 : (place + 1) * 256],
            basis_ref[place],
            preferred_element_type=f32,
        )
    out_ref[...] = jnp.broadcast_to(acc.T.astype(bf16), (4, 128, 256))


def gradient_kernel(halves_ref, cotangent_ref, out_ref, parts, sems):
    copies = []
    for g in range(2):
        both = halves_ref[g]
        for piece in range(2):
            rows = slice(piece * 8, piece * 8 + 8)
            part = jnp.dot(
                both[piece * 128 : piece * 128 + 128],
                cotangent_ref[g],
                preferred_element_type=f32,
            )
            parts[rows, g] = part.astype(bf16).reshape(8, 16, 896)
            copies.append(
                pltpu.make_async_copy(
                    parts.at[rows, g], out_ref.at[rows, g], sems.at[2 * g + piece]
                )
            )
            copies[-1].start()
    for copy in copies:
        copy.wait()


def gradient_parts(halves, cotangent):
    out = jax.ShapeDtypeStruct((16, 2, 16, 896), bf16)
    return pl.pallas_call(
        gradient_kernel,
        in_specs=[pl.BlockSpec(memory_space=pltpu.VMEM)] * 2,
        out_specs=pl.BlockSpec(memory_space=pl.ANY),
        out_shape=out,
        scratch_shapes=[pltpu.VMEM(out.shape, bf16), pltpu.SemaphoreType.DMA((4,))],
        compiler_params=pltpu.CompilerParams(vmem_limit_bytes=16 * 2**20),
        name="gradient_parts",
    )(halves, cotangent)


def update_kernel(basis_ref, steps_ref, gradient_ref, first_ref, second_ref, *refs):
    outs, (update, first, second, sems) = refs[:3], refs[3:]
    gradient = gradient_ref[...]
    first[...] = 0.9 * first_ref[...] + 0.1 * gradient
    second[...] = 0.999 * second_ref[...] + 0.001 * gradient * gradient
    copies = [
        pltpu.make_async_copy(first, outs[1], sems.at[4]),
        pltpu.make_async_copy(second, outs[2], sems.at[5]),
    ]
    for copy in copies:
        copy.start()
    for g in range(2):
        steps = steps_ref[:, g].reshape(256, 896)
        for piece in range(2):
            rows = slice(piece * 128, piece * 128 + 128)
            update[g, rows] = jnp.dot(
                basis_ref[g, rows], steps, preferred_element_type=f32
            ).astype(bf16)
            copies.append(
                pltpu.make_async_copy(
                    update.at[g, rows], outs[0].at[g, rows], sems.at[2 * g + piece]
                )
            )
            copies[-1].start()
    for copy in copies:
        copy.wait()


def finish(basis, steps, gradient, first_moment, second_moment):
    outs = (
        jax.ShapeDtypeStruct((2, 256, 896), bf16),
        jax.ShapeDtypeStruct((2, 8, 896), f32),
        jax.ShapeDtypeStruct((2, 8, 896), f32),
    )
    return pl.pallas_call(
        update_kernel,
        in_specs=[pl.BlockSpec(memory_space=pltpu.VMEM)] * 5,
        out_specs=(pl.BlockSpec(memory_space=pl.ANY),) * 3,
        out_shape=outs,
        scratch_shapes=[
            *(pltpu.VMEM(out.shape, out.dtype) for out in outs),
            pltpu.SemaphoreType.DMA((6,)),
        ],
        compiler_params=pltpu.CompilerParams(vmem_limit_bytes=16 * 2**20),
        name="finish",
    )(basis, steps, gradient, first_moment, second_moment)


def per_device(inputs, cotangent, subspace, first_moment, second_moment):
    half, core = lax.axis_index("z_hi"), lax.axis_index("core")
    low = lax.axis_index("z_lo")
    across = lax.axis_index("z_mid") == lax.axis_index("z_top")

    order = lax.broadcasted_iota(jnp.int32, (256,), 0)
    order = order // 8 % 2 * 128 + order // 16 * 8 + order % 8
    wanted = lax.dynamic_slice(order, (jnp.where(across, 1 - low, low) * 128,), (128,))
    every = lax.broadcasted_iota(jnp.int32, (128, 256), 1)
    pick = (wanted[:, None] == every).astype(bf16)
    chosen = lax.dynamic_index_in_dim(subspace, core, 0, keepdims=False)
    mine = jnp.einsum("dr,sr->ds", chosen, pick, preferred_element_type=f32).astype(bf16)
    theirs = lax.ppermute(mine, LINE, [(z, 15 - z) for z in (0, 1, 6, 7, 8, 9, 14, 15)])
    moments = jnp.stack([first_moment, second_moment])
    moments_far = lax.ppermute(moments.astype(bf16), "z_hi", SWAP)
    features = jnp.where(across, 1 - half, half) * 4096
    held = fetch(inputs, features)
    basis = jnp.where(across, theirs, mine)
    basis, held = lax.optimization_barrier((basis, held))

    basis = spread(basis, PLANE, 16)
    projected = in_vmem(
        project_kernel, jax.ShapeDtypeStruct((4, 128, 256), bf16), "project", basis, held
    )
    projected = lax.all_to_all(projected, NEAR, 0, 0, tiled=True)
    projected = jnp.sum(projected.reshape(2, 256, 256).astype(f32), axis=0).astype(bf16)
    projected = lax.all_gather(projected, "core", axis=0)
    partial = gradient_parts(projected, cotangent)
    parts = lax.all_to_all(partial, PLANE, 0, 0, tiled=True)
    own = jnp.sum(parts.astype(f32), axis=0).reshape(2, 2, 8, 896)
    sums = lax.all_gather(own.astype(bf16), "z_hi", axis=0)
    sums, moments_far = lax.optimization_barrier((sums, moments_far))
    moments_far = moments_far.astype(f32)
    after, _ = lax.optimization_barrier((subspace, own))
    move = (order[:, None] == lax.broadcasted_iota(jnp.int32, (256, 256), 1)).astype(bf16)
    ordered = jnp.einsum("gdr,sr->gds", after, move, preferred_element_type=f32).astype(bf16)
    gradient = own + jnp.where(half == 0, sums[1], sums[0]).astype(f32)

    near_far = jnp.stack([moments, moments_far], axis=2)
    far_near = jnp.stack([moments_far, moments], axis=2)
    held = jnp.where(half == 0, near_far, far_near)
    first_fix = 1.0 - 0.9**STEP
    second_fix = 1.0 - 0.999**STEP
    new_first = 0.9 * held[0] + 0.1 * gradient
    new_second = 0.999 * held[1] + 0.001 * gradient * gradient
    normalized = new_first / first_fix / (jnp.sqrt(new_second / second_fix) + 1e-08)
    gradient = lax.dynamic_index_in_dim(gradient, half, 1, keepdims=False)
    normalized, gradient, ordered = lax.optimization_barrier(
        (normalized.astype(bf16).reshape(2, 16, 896), gradient, ordered)
    )
    steps = spread(normalized, PLANE, 16)
    return finish(ordered, steps, gradient, first_moment, second_moment)


def solution(mesh):
    fine = Mesh(
        mesh.devices.reshape(2, 4, 4, 2, 2, 2, 2),
        ("z_hi", "y", "x", "z_top", "z_mid", "z_lo", "core"),
    )
    dp, shard = ("z_hi", "y", "x"), ("z_top", "z_mid", "z_lo", "core")
    return jax.shard_map(
        per_device,
        mesh=fine,
        in_specs=(
            P(dp, None),
            P(None, dp, shard),
            P(None, dp, None),
            P(None, dp, shard),
            P(None, dp, shard),
        ),
        out_specs=(P(None, dp, shard), P(None, dp, shard), P(None, dp, shard)),
        check_vma=False,
    )
```
